128 devices in a mesh: node: 8 (over z, core), local: 16 (over x, y).
Axes of the slice: x: 4, y: 4, z: 4, core: 2. Of those that a mesh axis runs over, the one named last changes fastest.
Arguments:
- tokens: bfloat16 [16384, 2048], P(('node', 'local')), may hold values from -6 to 6
- expert_ids: int32 [16384, 8], P(('node', 'local')), may hold values from 0 to 127, as said below
- gate_weights: bfloat16 [16384, 8], P(('node', 'local')), may hold values from 0.099609375 to 1
- slot_map: int32 [128], replicated, may hold values from 0 to 15, as said below
- w_gate: bfloat16 [128, 2048, 768], P(('node', 'local')), may hold values from -0.125 to 0.125
- w_up: bfloat16 [128, 2048, 768], P(('node', 'local')), may hold values from -0.125 to 0.125
- w_down: bfloat16 [128, 768, 2048], P(('node', 'local')), may hold values from -0.21875 to 0.21875
Outputs:
- layer_out: bfloat16 [16384, 2048], P(('node', 'local'))
The draws below stay inside these ranges and needn't reach their ends.
Inputs may be any that keep to these rules, and one draw needn't show every extreme that they name: `expert_ids`: each token names 8 different experts lying in at most 4 groups (expert e lies in group e // 16); how many of them fall in one group varies from token to token. In each device's block of 128 tokens no expert is named by more than 24 tokens; one group, the same for every block and drawn from the seed, is named by every token, and one of its experts by exactly 24 tokens of every block. Within each group a permutation of the local indices: expert e is served by the device of node e // 16 and local index slot_map[e].
All inputs are finite; a program needn't handle non-finite values.
Results may differ from the reference program's by a relative error of at most 0.012.
Values may be sent and summed in bfloat16 or wider, within the bound.
No kernel may reach another device: no remote copies, remote signals or barrier semaphores. Data moves between devices by JAX's collectives and lax.ppermute only.
A program may use at most 128 MiB of HBM per device.

```python
import math
import jax
import jax.numpy as jnp
from jax import lax

D = 2048
FF = 768
TOK_DEV = 128
GROUPS = 8
GROUP_EXP = 16
EXPERTS = 128
GPICK = 4
TOPK = 8
EXP_ROWS = 3072
TOKENS = 16384


def distinct_order(key, shape, spread, bias):
    noise = jax.random.randint(key, shape, 0, spread)
    last_len = shape[-1]
    score = (bias + noise) * last_len + jnp.arange(last_len, dtype=jnp.int32)
    return jnp.argsort(-score, axis=-1).astype(jnp.int32)


def draw_expert_ids(key, part):
    key = jax.random.fold_in(key, 7)
    keys = jax.random.split(key, 8)
    blocks = TOKENS // TOK_DEV
    rest = GPICK - 1
    hot_group = jax.random.randint(keys[0], (), 0, GROUPS)
    heavy = jax.random.randint(keys[1], (blocks,), 0, TOK_DEV // 4 + 1)
    short = jax.random.randint(keys[2], (blocks,), 0, GROUP_EXP)
    light = 2 * heavy + short
    rank = distinct_order(keys[3], (blocks, TOK_DEV), 1 << 20, 0)
    more = (rank < heavy[:, None]).astype(jnp.int32)
    fewer = ((rank >= heavy[:, None]) & (rank < light[:, None])).astype(jnp.int32)
    hot_count = 3 + more - fewer
    remain = TOPK - hot_count
    slot_ids = jnp.arange(rest, dtype=jnp.int32)
    base = remain[:, :, None] // rest + (slot_ids[None, None, :] < (remain % rest)[:, :, None]).astype(jnp.int32)
    pair_total = rest // 2
    if pair_total > 0:
        move = jax.random.randint(keys[4], (blocks, TOK_DEV, pair_total), -1, 2)
        delta = jnp.stack([move, -move], axis=3).reshape(blocks, TOK_DEV, 2 * pair_total)
        delta = jnp.concatenate([delta, jnp.zeros((blocks, TOK_DEV, rest - 2 * pair_total), jnp.int32)], axis=2)
        base = base + delta
    group_bias = jax.random.randint(keys[6], (GROUPS - 1,), 0, 3) * 32
    other_order = distinct_order(keys[5], (blocks, TOK_DEV, GROUPS - 1), 64, group_bias[None, None, :])
    other_group = (hot_group + 1 + other_order[:, :, :rest]) % GROUPS
    hot_column = jnp.full((blocks, TOK_DEV, 1), hot_group, jnp.int32)
    slot_group = jnp.concatenate([hot_column, other_group], axis=2).astype(jnp.int32)
    slot_count = jnp.concatenate([hot_count[:, :, None], base], axis=2).astype(jnp.int32)
    group_cols = jnp.arange(GROUPS, dtype=jnp.int32)
    per_group = jnp.sum(slot_count[:, :, :, None] * (slot_group[:, :, :, None] == group_cols[None, None, None, :]).astype(jnp.int32), axis=2)
    group_start = jnp.cumsum(per_group, axis=2) - per_group
    token_base = jnp.cumsum(per_group, axis=1) - per_group
    slot_start = jnp.take_along_axis(group_start, slot_group, axis=2)
    slot_end = jnp.cumsum(slot_count, axis=2)
    entry = jnp.arange(TOPK, dtype=jnp.int32)
    slot_of = jnp.sum(entry[None, None, :, None] >= slot_end[:, :, None, :], axis=3).astype(jnp.int32)
    first_entry = jnp.take_along_axis(slot_end - slot_count, slot_of, axis=2)
    group_at = jnp.take_along_axis(slot_group, slot_of, axis=2)
    position = jnp.take_along_axis(slot_start, slot_of, axis=2) + entry[None, None, :] - first_entry
    within = position - jnp.take_along_axis(group_start, group_at, axis=2)
    running = jnp.take_along_axis(token_base, group_at, axis=2) + within
    member_order = distinct_order(keys[7], (blocks, GROUPS, GROUP_EXP), 1 << 16, 0).reshape(blocks, GROUPS * GROUP_EXP)
    lookup = (group_at * GROUP_EXP + running % GROUP_EXP).reshape(blocks, TOK_DEV * TOPK)
    member = jnp.take_along_axis(member_order, lookup, axis=1).reshape(blocks, TOK_DEV, TOPK)
    chosen = group_at * GROUP_EXP + member
    entry_order = distinct_order(jax.random.fold_in(key, 5), (blocks, TOK_DEV, TOPK), 64, 0)
    chosen = jnp.take_along_axis(chosen, entry_order, axis=2)
    return chosen.reshape(TOKENS, TOPK).astype(jnp.int32)


def draw_slot_map(key, part):
    key = jax.random.fold_in(key, 19)
    slots = distinct_order(key, (GROUPS, GROUP_EXP), 1 << 16, 0)
    return slots.reshape(EXPERTS).astype(jnp.int32)


def block_scale(rng, dims, cuts, least, high):
    loudness, own = 1.0, jax.random.fold_in(rng, 6)
    for dim, blocks in cuts:
        steps = jnp.exp(jax.random.uniform(jax.random.fold_in(own, dim), (blocks,), jnp.float32, least / len(cuts), high / len(cuts)))
        loudness = loudness * jnp.repeat(steps, dims[dim] // blocks).reshape([-1 if axis == dim else 1 for axis in range(len(dims))])
    return loudness


def centred(key, dims, deviation, bound, shards=(), kind=jnp.bfloat16):
    factor_of = block_scale(key, dims, shards, -0.22, 0.18) if shards else 1.0
    entries = jax.random.normal(key, dims, jnp.float32) * deviation * factor_of
    return jnp.minimum(jnp.maximum(entries, -bound), bound).astype(kind)


def setup_inputs(seed: int = 0) -> dict:
    key_list = jax.random.split(jax.random.key(seed), 8)
    return {
        "tokens": centred(key_list[0], (TOKENS, D), 1.0, 6.0, ((0, 128),)),
        "expert_ids": draw_expert_ids(jax.random.fold_in(key_list[7], 71), 0),
        "gate_weights": jnp.clip(jnp.exp(math.log(1.0) - 2.306499 * jax.random.uniform(key_list[2], (TOKENS, TOPK), jnp.float32) ** block_scale(key_list[2], (TOKENS, TOPK), ((0, 128),), -0.2, 0.2)), 0.099609375, 1.0).astype(jnp.bfloat16),
        "slot_map": draw_slot_map(jax.random.fold_in(key_list[7], 71), 0),
        "w_gate": centred(key_list[4], (EXPERTS, D, FF), D ** -0.5, 0.125, ((0, 128),)),
        "w_up": centred(key_list[5], (EXPERTS, D, FF), D ** -0.5, 0.125, ((0, 128),)),
        "w_down": centred(key_list[6], (EXPERTS, FF, D), FF ** -0.5, 0.21875, ((0, 128),)),
    }


row_block = 512


def expert_rows(token_rows, gate_mat, up_mat, down_mat):
    gate_part = jnp.dot(token_rows, gate_mat, preferred_element_type=jnp.float32)
    up_part = jnp.dot(token_rows, up_mat, preferred_element_type=jnp.float32)
    hidden = (jax.nn.silu(gate_part) * up_part).astype(jnp.bfloat16)
    return jnp.dot(hidden, down_mat, preferred_element_type=jnp.float32).astype(jnp.bfloat16)


def reference(tokens, expert_ids, gate_weights, slot_map, w_gate, w_up, w_down):
    entry_count = TOKENS * TOPK
    holder = (expert_ids // GROUP_EXP) * GROUP_EXP + slot_map[expert_ids]
    holder_flat = holder.reshape(-1).astype(jnp.int32)
    sort_order = jnp.argsort(holder_flat, stable=True).astype(jnp.int32)
    counts = jnp.zeros((EXPERTS,), jnp.int32).at[holder_flat].add(1)
    offsets = (jnp.cumsum(counts) - counts).astype(jnp.int32)
    sorted_tokens = jnp.concatenate([sort_order // TOPK, jnp.full((row_block,), TOKENS, jnp.int32)])
    padded = jnp.concatenate([tokens, jnp.zeros((1, D), tokens.dtype)], axis=0)
    sub_count = -(-EXP_ROWS // row_block)

    def expert_step(carry, block_index):
        expert = block_index // sub_count
        row_start = offsets[expert] + (block_index % sub_count) * row_block

        def run_block(outputs):
            picked = lax.dynamic_slice(sorted_tokens, (row_start,), (row_block,))
            result = expert_rows(padded[picked], w_gate[expert], w_up[expert], w_down[expert])
            return lax.dynamic_update_slice(outputs, result, (row_start, jnp.int32(0)))

        def keep_block(outputs):
            return outputs

        live = (block_index % sub_count) * row_block < counts[expert]
        return lax.cond(live, run_block, keep_block, carry), None

    blank = jnp.zeros((entry_count + row_block, D), jnp.bfloat16)
    outputs, unused = lax.scan(expert_step, blank, jnp.arange(EXPERTS * sub_count, dtype=jnp.int32))
    expert_out = jnp.zeros((entry_count, D), jnp.bfloat16).at[sort_order].set(outputs[:entry_count])
    expert_out = expert_out.reshape(TOKENS, TOPK, D).astype(jnp.float32)
    group_cols = jnp.arange(GROUPS, dtype=jnp.int32)
    select = (expert_ids // GROUP_EXP)[:, :, None] == group_cols[None, None, :]
    weights = jnp.where(select, gate_weights.astype(jnp.float32)[:, :, None], jnp.float32(0.0))
    group_sum = jnp.einsum("tkg,tkd->tgd", weights, expert_out).astype(jnp.bfloat16)
    return jnp.sum(group_sum.astype(jnp.float32), axis=1).astype(jnp.bfloat16)
```

```python
import jax
import jax.numpy as jnp
from jax import lax
from jax.sharding import PartitionSpec as P

BF = jnp.bfloat16
F32 = jnp.float32
AXES = ("node", "local")


def dot(a, b):
    return jnp.dot(a, b, preferred_element_type=F32)


def strict_lower(n):
    rows = lax.broadcasted_iota(jnp.int32, (n, n), 0)
    cols = lax.broadcasted_iota(jnp.int32, (n, n), 1)
    return (cols < rows).astype(BF)


def ranks(weights, blocks):
    named = weights > 0
    ones = named.astype(BF).reshape(blocks, -1, weights.shape[1])
    inside = jnp.einsum("ts,bsl->btl", strict_lower(ones.shape[1]), ones, preferred_element_type=F32)
    if blocks > 1:
        totals = jnp.sum(ones.astype(F32), axis=1)
        before = jnp.cumsum(totals, axis=0) - totals
        inside = inside + before[:, None, :]
    rank = inside.reshape(weights.shape).astype(jnp.int32)
    return jnp.where(named, rank, -1)


def pick_matrix(rank, capacity):
    tokens, holders = rank.shape
    slots = lax.broadcasted_iota(jnp.int32, (holders, capacity, tokens), 1)
    return (rank.T[:, None, :] == slots).astype(BF).reshape(holders * capacity, tokens)


def combine_matrix(rank, weights, capacity):
    tokens, holders = rank.shape
    slots = lax.broadcasted_iota(jnp.int32, (tokens, holders, capacity), 2)
    spread = jnp.where(rank[:, :, None] == slots, weights[:, :, None], jnp.zeros((), BF))
    return spread.reshape(tokens, holders * capacity)


def exchange(rows):
    return lax.all_to_all(rows, "local", split_axis=0, concat_axis=0, tiled=True)


def hidden_rows(rows, gate_mat, up_mat):
    return (jax.nn.silu(dot(rows, gate_mat)) * dot(rows, up_mat)).astype(BF)


def body(tokens, expert_ids, gate_weights, slot_map, w_gate, w_up, w_down):
    tok, width = tokens.shape
    ff = w_gate.shape[2]
    nodes, locals_ = lax.axis_size("node"), lax.axis_size("local")
    experts = slot_map.shape[0]
    zs = nodes // 2
    node = lax.axis_index("node")
    z, core = node // 2, node % 2
    hot_cap = 3 * tok // locals_
    full_cap = hot_cap * nodes
    caps = [0] + [c for c in range(16, 129, 16) if c < full_cap] + [160, full_cap]
    caps = sorted({c for c in caps if c <= full_cap})

    def along(dz):
        return [(a * 2 + b, ((a + dz) % zs) * 2 + b) for a in range(zs) for b in range(2)]

    swap_pairs = [(a, a ^ 1) for a in range(nodes)]

    def shift(x, dz):
        return lax.ppermute(x, "node", along(dz))

    def swap(x):
        return lax.ppermute(x, "node", swap_pairs)

    mine = [tokens, shift(tokens, 1), shift(tokens, 3), shift(tokens, 2)]
    offsets = (0, -1, 1, 2)
    own_core = jnp.concatenate(mine, axis=0)
    column = jnp.concatenate([own_core, swap(own_core)], axis=0)

    expert_cols = jnp.arange(experts, dtype=jnp.int32)
    spread = jnp.sum(
        jnp.where(expert_ids[:, :, None] == expert_cols, gate_weights[:, :, None].astype(F32), 0.0), axis=1
    ).astype(BF)
    holder = (expert_cols // locals_) * locals_ + slot_map
    place = (holder[:, None] == expert_cols[None, :]).astype(BF)
    by_holder = dot(spread, place).astype(BF)
    column_weights = lax.all_gather(by_holder, "node", axis=0, tiled=False)

    counts = jnp.sum((by_holder > 0).astype(jnp.int32), axis=0)
    table = lax.all_to_all(
        jnp.broadcast_to(counts[None, :], (nodes * locals_, experts)), AXES, split_axis=0, concat_axis=0, tiled=True
    )
    per_column = jnp.sum(table.reshape(nodes, locals_, experts), axis=0)
    group_rows = jnp.sum(per_column.reshape(locals_, nodes, locals_), axis=(0, 2))
    group_need = jnp.max(per_column.reshape(locals_, nodes, locals_), axis=(0, 2))
    hot = jnp.argmax(group_rows).astype(jnp.int32)
    node_cols = jnp.arange(nodes, dtype=jnp.int32)
    is_hot_node = node == hot
    need = jnp.where(is_hot_node, 0, jnp.sum(jnp.where(node_cols == node, group_need, 0)))
    which = sum((need > c).astype(jnp.int32) for c in caps[:-1])

    hot_weights = lax.dynamic_slice(by_holder, (0, hot * locals_), (tok, locals_))
    hot_rank = ranks(hot_weights, 1)
    hot_out = dot(pick_matrix(hot_rank, hot_cap), tokens).astype(BF).reshape(locals_, hot_cap, width)
    hot_in = exchange(hot_out).reshape(locals_ * hot_cap, width)

    hot_z, hot_core = hot // 2, hot % 2
    rel = (z - hot_z) % zs
    same = core == hot_core
    mats = (w_gate[0], w_up[0], w_down[0])

    def first_step(mat):
        half = mat.shape[0] // 2
        other = swap(mat[half:])
        src = jnp.where(same, mat[:half], other)
        a, b = src[: half // 2], src[half // 2 :]
        return a, b, shift(a, 1), shift(b, 3)

    def second_step(a, b, a1, b1):
        plus = shift(jnp.where(rel == 0, b, a1), 1)
        minus = shift(jnp.where(rel == 0, a, b1), 3)
        return plus, minus

    def last_step(a, b, a1, b1, plus, minus):
        part_a = jnp.where(rel == 0, a, jnp.where(rel == 1, a1, jnp.where(rel == 3, minus, plus)))
        part_b = jnp.where(rel == 0, b, jnp.where(rel == 1, plus, jnp.where(rel == 3, b1, minus)))
        here = jnp.concatenate([part_a, part_b], axis=0)
        there = swap(here)
        low = jnp.where(same, here, there)
        high = jnp.where(same, there, here)
        return jnp.concatenate([low, high], axis=0)

    stage1 = [first_step(m) for m in mats]

    order = jnp.stack([((z + dz) % zs) * 2 + core for dz in offsets] + [((z + dz) % zs) * 2 + 1 - core for dz in offsets])
    plane_weights = lax.dynamic_slice(column_weights, (0, 0, node * locals_), (nodes, tok, locals_))
    plane_weights = plane_weights[order].reshape(nodes * tok, locals_)
    plane_weights = jnp.where(is_hot_node, jnp.zeros((), BF), plane_weights)
    plane_rank = ranks(plane_weights, nodes)
    rows_max = locals_ * full_cap

    def send(cap):
        def run(rank, rows, gate_mat, up_mat):
            if cap == 0:
                return jnp.zeros((rows_max, ff), BF)
            out = dot(pick_matrix(rank, cap), rows).astype(BF).reshape(locals_, cap, width)
            got = exchange(out).reshape(locals_ * cap, width)
            hid = hidden_rows(got, gate_mat, up_mat)
            return jnp.pad(hid, ((0, rows_max - locals_ * cap), (0, 0)))

        return run

    def back(cap):
        def run(hid, rank, weights, down_mat):
            if cap == 0:
                return jnp.zeros((nodes * tok, width), BF)
            out = dot(hid[: locals_ * cap], down_mat).astype(BF).reshape(locals_, cap, width)
            got = exchange(out).reshape(locals_ * cap, width)
            return dot(combine_matrix(rank, weights, cap), got).astype(BF)

        return run

    hid = lax.switch(which, [send(c) for c in caps], plane_rank, column, mats[0], mats[1])
    stage2 = [second_step(*s) for s in stage1]
    sums = lax.switch(which, [back(c) for c in caps], hid, plane_rank, plane_weights, mats[2])

    hot_mats = [last_step(*s, *t) for s, t in zip(stage1, stage2)]
    hot_hid = hidden_rows(hot_in, hot_mats[0], hot_mats[1])
    hot_res = dot(hot_hid, hot_mats[2]).astype(BF).reshape(locals_, hot_cap, width)
    hot_back = exchange(hot_res).reshape(locals_ * hot_cap, width)
    hot_sum = dot(combine_matrix(hot_rank, hot_weights, hot_cap), hot_back).astype(BF)

    half = zs * tok
    pair = (sums[:half].astype(F32) + swap(sums[half:]).astype(F32)).astype(BF).reshape(zs, tok, width)
    parts = [pair[0], shift(pair[1], 3), shift(pair[2], 1), shift(pair[3], 2), hot_sum]
    return sum(p.astype(F32) for p in parts).astype(BF)


def solution(mesh):
    rows = P(AXES, None)
    mats = P(AXES, None, None)
    return jax.shard_map(
        body,
        mesh=mesh,
        in_specs=(rows, rows, rows, P(), mats, mats, mats),
        out_specs=rows,
        check_vma=False,
    )
```

```python
import jax
import jax.numpy as jnp
from jax import lax
from jax.experimental import pallas as pl
from jax.experimental.pallas import tpu as pltpu
from jax.sharding import Mesh
from jax.sharding import PartitionSpec as P

BF = jnp.bfloat16
F32 = jnp.float32
ALL = ("z", "core", "local")
HALF = ("z", "local")
CAPS = (24, 32, 40)
SLOTS = 8
CHUNK = 256


def dot(a, b):
    return jnp.dot(a, b, preferred_element_type=F32)


def strict_lower(n):
    rows = lax.broadcasted_iota(jnp.int32, (n, n), 0)
    cols = lax.broadcasted_iota(jnp.int32, (n, n), 1)
    return (cols < rows).astype(BF)


def ranks(weights):
    named = weights > 0
    rank = dot(strict_lower(weights.shape[0]), named.astype(BF)).astype(jnp.int32)
    return jnp.where(named, rank, -1)


def pick_matrix(places, size):
    tokens, holders = places[0].shape
    slots = lax.broadcasted_iota(jnp.int32, (holders, size, tokens), 1)
    hits = places[0].T[:, None, :] == slots
    for place in places[1:]:
        hits = hits | (place.T[:, None, :] == slots)
    return hits.astype(BF).reshape(holders * size, tokens)


def combine_matrix(places, weights, size):
    tokens, holders = places[0].shape
    slots = lax.broadcasted_iota(jnp.int32, (tokens, holders, size), 2)
    spread = jnp.zeros((), BF)
    for place, weight in zip(places, weights):
        spread = jnp.where(place[:, :, None] == slots, weight[:, :, None], spread)
    return spread.reshape(tokens, holders * size)


def exchange(rows):
    return lax.all_to_all(rows, HALF, split_axis=0, concat_axis=0, tiled=True)


def after(x, *others):
    return lax.optimization_barrier((x, others))[0]


def hidden_of(gate, up):
    return jax.nn.silu(gate) * up


def expert_kernel(flags, rows, mask, *refs):
    sources, out, store, hidden, sems = refs[:6], refs[6], refs[7:13], refs[13:15], refs[15]
    step = pl.program_id(0)
    kind = flags[step]
    count, ff = hidden[0].shape
    width = rows.shape[2]

    def copy(i):
        return pltpu.make_async_copy(sources[i], store[i], sems.at[i])

    def arrive(*which):
        @pl.when(step == 0)
        def _():
            for i in which:
                copy(i).wait()

    @pl.when(step == 0)
    def _():
        for i in (0, 1, 3, 4, 2, 5):
            copy(i).start()

    def up(expert):
        mine = (mask[0][:, :1] > 0) == (expert == 0)

        @pl.loop(0, ff // CHUNK)
        def _(j):
            cols = pl.ds(pl.multiple_of(j * CHUNK, CHUNK), CHUNK)
            x = rows[...].reshape(count, width)
            act = hidden_of(dot(x, store[3 * expert][:, cols]), dot(x, store[3 * expert + 1][:, cols]))
            hidden[expert][:, cols] = jnp.where(mine, act, 0.0).astype(BF)

    arrive(0, 1)
    pl.when(kind % 2 == 1)(lambda: up(0))
    arrive(3, 4)
    pl.when(kind >= 2)(lambda: up(1))
    arrive(2, 5)

    def down(experts):
        @pl.loop(0, width // CHUNK)
        def _(j):
            cols = pl.ds(pl.multiple_of(j * CHUNK, CHUNK), CHUNK)
            total = sum(dot(hidden[e][...], store[3 * e + 2][:, cols]) for e in experts)
            out[:, :, cols] = total.astype(BF).reshape(out.shape[0], out.shape[1], CHUNK)

    @pl.when(kind == 0)
    def _():
        out[...] = jnp.zeros_like(out)

    pl.when(kind == 1)(lambda: down([0]))
    pl.when(kind == 2)(lambda: down([1]))
    pl.when(kind == 3)(lambda: down([0, 1]))


def tile_plan(first_rows, all_rows, cap):
    sources, tiles, lanes = first_rows.shape[0], cap // SLOTS, 128
    slots = lax.broadcasted_iota(jnp.int32, (tiles, sources, SLOTS), 0) * SLOTS
    slots = slots + lax.broadcasted_iota(jnp.int32, (tiles, sources, SLOTS), 2)
    is_first = (slots < first_rows[None, :, None]).reshape(tiles, sources * SLOTS)
    any_row = (slots < all_rows[None, :, None]).reshape(tiles, sources * SLOTS)
    flags = jnp.any(is_first, axis=1).astype(jnp.int32) + 2 * jnp.any(any_row & ~is_first, axis=1).astype(jnp.int32)
    return flags, jnp.broadcast_to(is_first.astype(F32)[:, :, None], (tiles, sources * SLOTS, lanes))


def two_experts(flags, mask, rows, first, second):
    sources, cap, width = rows.shape
    ff = first[0].shape[1]
    count = sources * SLOTS
    block = pl.BlockSpec((sources, SLOTS, width), lambda i, f: (0, i, 0))
    return pl.pallas_call(
        expert_kernel,
        out_shape=pltpu.HBM(rows.shape, BF),
        grid_spec=pltpu.PrefetchScalarGridSpec(
            num_scalar_prefetch=1,
            grid=(cap // SLOTS,),
            in_specs=[block, pl.BlockSpec((1,) + mask.shape[1:], lambda i, f: (i, 0, 0))]
            + [pl.BlockSpec(memory_space=pl.ANY)] * 6,
            out_specs=block,
            scratch_shapes=[pltpu.VMEM(m.shape, BF) for m in first + second]
            + [pltpu.VMEM((count, ff), BF)] * 2
            + [pltpu.SemaphoreType.DMA((6,))],
        ),
        compiler_params=pltpu.CompilerParams(vmem_limit_bytes=48 * 2**20),
        cost_estimate=pl.CostEstimate(
            flops=6 * sources * cap * width * ff, bytes_accessed=12 * width * ff + 4 * sources * cap * width, transcendentals=0
        ),
    )(flags, rows, mask, *first, *second)


def body(tokens, expert_ids, gate_weights, slot_map, w_gate, w_up, w_down):
    tok, width = tokens.shape
    zs, locals_ = lax.axis_size("z"), lax.axis_size("local")
    chips = zs * locals_
    experts = slot_map.shape[0]
    z, core, local = (lax.axis_index(a) for a in ALL)
    full = 2 * (3 * tok // locals_)

    own = (w_gate[0], w_up[0], w_down[0])
    sib = tuple(lax.ppermute(m, "core", [(0, 1), (1, 0)]) for m in own)

    expert_cols = jnp.arange(experts, dtype=jnp.int32)
    spread = jnp.sum(
        jnp.where(expert_ids[:, :, None] == expert_cols, gate_weights[:, :, None].astype(F32), 0.0), axis=1
    ).astype(BF)
    holder = (expert_cols // locals_) * locals_ + slot_map
    place = (holder[:, None] == expert_cols[None, :]).astype(BF)
    by_holder = dot(spread, place).astype(BF)
    counts = jnp.sum((by_holder > 0).astype(jnp.int32), axis=0)
    table = lax.all_to_all(
        jnp.broadcast_to(counts[None, :], (2 * chips, experts)), ALL, split_axis=0, concat_axis=0, tiled=True
    )

    by_core = by_holder.reshape(tok, zs, 2, locals_)
    even, odd = (by_core[:, :, i, :].reshape(tok, chips) for i in (0, 1))
    weights = [jnp.where(core == 0, even, odd), jnp.where(core == 0, odd, even)]
    rank_own, rank_sib = ranks(weights[0]), ranks(weights[1])
    own_count = jnp.sum((rank_own >= 0).astype(jnp.int32), axis=0)
    places = [rank_own, jnp.where(rank_sib >= 0, rank_sib + own_count[None, :], -1)]

    table = table.reshape(zs, 2, locals_, zs, 2, locals_)
    need = jnp.max(jnp.sum(table, axis=4))
    here = jnp.sum(jnp.where(jnp.arange(2)[:, None, None, None, None] == core, table, 0), axis=1).reshape(chips, zs, 2, locals_)
    place_here = (jnp.arange(zs)[:, None, None] == z) & (jnp.arange(locals_)[None, None, :] == local)
    here = jnp.sum(jnp.where(place_here, here, 0), axis=(1, 3))
    all_rows = here[:, 0] + here[:, 1]
    own_rows = jnp.where(core == 0, here[:, 0], here[:, 1])

    def layer(cap):
        def run(tokens, places, weights, own_rows, all_rows, own, sib):
            spread = combine_matrix(places, weights, cap)
            flags, mask = tile_plan(own_rows, all_rows, cap)
            send = dot(pick_matrix(places, cap), tokens).astype(BF).reshape(chips, cap, width)
            send, spread, flags, mask, sib = lax.optimization_barrier((send, spread, flags, mask, sib))
            out = two_experts(flags, mask, exchange(send), own, sib)
            return dot(spread, exchange(out).reshape(-1, width)).astype(BF)

        return run

    caps = [c for c in CAPS if c < full] + [full]
    which = sum((need > c).astype(jnp.int32) for c in caps[:-1])
    return lax.switch(which, [layer(c) for c in caps], tokens, places, weights, own_rows, all_rows, own, sib)


def solution(mesh):
    halves = Mesh(mesh.devices.reshape(-1, 2, mesh.devices.shape[1]), ALL)
    rows = P(ALL, None)
    mats = P(ALL, None, None)
    return jax.shard_map(
        body,
        mesh=halves,
        in_specs=(rows, rows, rows, P(), mats, mats, mats),
        out_specs=rows,
        check_vma=False,
    )
```

```python
import jax
import jax.numpy as jnp
from jax import lax
from jax.experimental import pallas as pl
from jax.experimental.pallas import tpu as pltpu
from jax.sharding import Mesh
from jax.sharding import PartitionSpec as P

BF = jnp.bfloat16
F32 = jnp.float32
ALL = ("z", "core", "local")
HALF = ("z", "local")
CAPS = (24, 32, 40)
SLOTS = 8
NARROW, WIDE = 256, 1024


def dot(a, b):
    return jnp.dot(a, b, preferred_element_type=F32)


def ranks(weights):
    named = weights > 0
    tokens = weights.shape[1]
    earlier = lax.broadcasted_iota(jnp.int32, (tokens, tokens), 0) < lax.broadcasted_iota(jnp.int32, (tokens, tokens), 1)
    rank = dot(named.astype(BF), earlier.astype(BF)).astype(jnp.int32)
    return jnp.where(named, rank, -1)


def slot_matrix(places, values, size):
    holders, tokens = places[0].shape
    slots = lax.broadcasted_iota(jnp.int32, (holders, size, tokens), 1)
    out = jnp.zeros((), BF)
    for place, value in zip(places, values):
        out = jnp.where(place[:, None, :] == slots, value[:, None, :], out)
    return out.reshape(holders * size, tokens)


def exchange(rows):
    return lax.all_to_all(rows, HALF, split_axis=0, concat_axis=0, tiled=True)


def after(x, *others):
    return lax.optimization_barrier((x, others))[0]


def hidden_of(gate, up):
    return jax.nn.silu(gate) * up


def expert_kernel(flags, rows, mask, *refs):
    sources, out, mats, hidden, sems = refs[:6], refs[6], refs[7:10], refs[10], refs[11]
    step = pl.program_id(0)
    kind = flags[step]
    count, width = hidden.shape[1], rows.shape[2]
    gate, up, down = mats

    def copy(i):
        return pltpu.make_async_copy(sources[i], mats[i % 3].at[i // 3], sems.at[i])

    def arrive(*which):
        @pl.when(step == 0)
        def _():
            for i in which:
                copy(i).wait()

    @pl.when(step == 0)
    def _():
        for i in (0, 1, 3, 4, 2, 5):
            copy(i).start()

    arrive(0, 1, 3, 4)

    @pl.loop(0, 2)
    def _(expert):
        @pl.when((kind == expert + 1) | (kind == 3))
        def _():
            mine = (mask[0][:, :1] > 0) == (expert == 0)

            @pl.loop(0, hidden.shape[2] // NARROW)
            def _(j):
                cols = pl.ds(pl.multiple_of(j * NARROW, NARROW), NARROW)
                x = rows[...].reshape(count, width)
                act = hidden_of(dot(x, gate[expert, :, cols]), dot(x, up[expert, :, cols]))
                hidden[expert, :, cols] = jnp.where(mine, act, 0.0).astype(BF)

    arrive(2, 5)

    def write(product):
        @pl.loop(0, width // WIDE)
        def _(j):
            cols = pl.ds(pl.multiple_of(j * WIDE, WIDE), WIDE)
            out[:, :, cols] = product(cols).astype(BF).reshape(out.shape[0], out.shape[1], WIDE)

    def one(expert):
        return lambda cols: dot(hidden[expert], down[expert, :, cols])

    @pl.when(kind == 0)
    def _():
        out[...] = jnp.zeros_like(out)

    pl.when((kind == 1) | (kind == 2))(lambda: write(one(jnp.maximum(kind, 1) - 1)))
    pl.when(kind == 3)(lambda: write(lambda cols: one(0)(cols) + one(1)(cols)))


def tile_plan(first_rows, all_rows, cap):
    sources, tiles, lanes = first_rows.shape[0], cap // SLOTS, 128
    slots = lax.broadcasted_iota(jnp.int32, (tiles, sources, SLOTS), 0) * SLOTS
    slots = slots + lax.broadcasted_iota(jnp.int32, (tiles, sources, SLOTS), 2)
    is_first = (slots < first_rows[None, :, None]).reshape(tiles, sources * SLOTS)
    any_row = (slots < all_rows[None, :, None]).reshape(tiles, sources * SLOTS)
    flags = jnp.any(is_first, axis=1).astype(jnp.int32) + 2 * jnp.any(any_row & ~is_first, axis=1).astype(jnp.int32)
    return flags, jnp.broadcast_to(is_first.astype(F32)[:, :, None], (tiles, sources * SLOTS, lanes))


def two_experts(flags, mask, rows, first, second):
    sources, cap, width = rows.shape
    ff = first[0].shape[1]
    count = sources * SLOTS
    block = pl.BlockSpec((sources, SLOTS, width), lambda i, f: (0, i, 0))
    return pl.pallas_call(
        expert_kernel,
        out_shape=pltpu.HBM(rows.shape, BF),
        grid_spec=pltpu.PrefetchScalarGridSpec(
            num_scalar_prefetch=1,
            grid=(cap // SLOTS,),
            in_specs=[block, pl.BlockSpec((1,) + mask.shape[1:], lambda i, f: (i, 0, 0))]
            + [pl.BlockSpec(memory_space=pl.ANY)] * 6,
            out_specs=block,
            scratch_shapes=[pltpu.VMEM((2,) + m.shape, BF) for m in first]
            + [pltpu.VMEM((2, count, ff), BF), pltpu.SemaphoreType.DMA((6,))],
        ),
        compiler_params=pltpu.CompilerParams(vmem_limit_bytes=40 * 2**20),
        cost_estimate=pl.CostEstimate(
            flops=6 * sources * cap * width * ff, bytes_accessed=12 * width * ff + 4 * sources * cap * width, transcendentals=0
        ),
    )(flags, rows, mask, *first, *second)


def body(tokens, expert_ids, gate_weights, slot_map, w_gate, w_up, w_down):
    tok, width = tokens.shape
    zs, locals_ = lax.axis_size("z"), lax.axis_size("local")
    chips = zs * locals_
    experts = slot_map.shape[0]
    z, core, local = (lax.axis_index(a) for a in ALL)
    full = 2 * (3 * tok // locals_)

    own = (w_gate[0], w_up[0], w_down[0])
    sib = tuple(lax.ppermute(m, "core", [(0, 1), (1, 0)]) for m in own)

    expert_rows = jnp.arange(experts, dtype=jnp.int32)
    ids, gates = expert_ids.T, gate_weights.T.astype(F32)
    spread = jnp.sum(jnp.where(ids[:, None, :] == expert_rows[:, None], gates[:, None, :], 0.0), axis=0).astype(BF)
    holder = (expert_rows // locals_) * locals_ + slot_map
    place = (expert_rows[:, None] == holder[None, :]).astype(BF)
    by_holder = dot(place, spread).astype(BF)
    counts = jnp.sum((by_holder > 0).astype(jnp.int32), axis=1)
    my_need = jnp.max(jnp.sum(counts.reshape(zs, 2, locals_), axis=1))
    message = jnp.stack([counts, jnp.broadcast_to(my_need, counts.shape)])
    table = lax.all_to_all(
        jnp.broadcast_to(message[None], (2 * chips, 2, experts)), ALL, split_axis=0, concat_axis=0, tiled=True
    )
    need = jnp.max(table[:, 1])

    by_core = by_holder.reshape(zs, 2, locals_, tok)
    even, odd = (by_core[:, i].reshape(chips, tok) for i in (0, 1))
    weights = [jnp.where(core == 0, even, odd), jnp.where(core == 0, odd, even)]
    rank_own, rank_sib = ranks(weights[0]), ranks(weights[1])
    own_count = jnp.sum((rank_own >= 0).astype(jnp.int32), axis=1, keepdims=True)
    places = [rank_own, jnp.where(rank_sib >= 0, rank_sib + own_count, -1)]

    cells = table[:, 0].reshape(zs, 2, locals_, experts)
    cells = jnp.where(core == 0, cells[:, 0], cells[:, 1]).reshape(chips, experts)
    node = z * 2 + core
    own_rows, sib_rows = (
        jnp.sum(jnp.where(expert_rows == n * locals_ + local, cells, 0), axis=1) for n in (node, node + 1 - 2 * core)
    )
    all_rows = own_rows + sib_rows

    def layer(cap):
        def run(tokens, places, weights, own_rows, all_rows, own, sib):
            spread = slot_matrix(places, weights, cap)
            flags, mask = tile_plan(own_rows, all_rows, cap)
            send = dot(slot_matrix(places, [jnp.ones_like(w) for w in weights], cap), tokens).astype(BF)
            send, spread, flags, mask, sib = lax.optimization_barrier((send, spread, flags, mask, sib))
            out = two_experts(flags, mask, exchange(send.reshape(chips, cap, width)), own, sib)
            return dot(spread.T, exchange(out).reshape(-1, width)).astype(BF)

        return run

    caps = [c for c in CAPS if c < full] + [full]
    which = sum((need > c).astype(jnp.int32) for c in caps[:-1])
    return lax.switch(which, [layer(c) for c in caps], tokens, places, weights, own_rows, all_rows, own, sib)


def solution(mesh):
    halves = Mesh(mesh.devices.reshape(-1, 2, mesh.devices.shape[1]), ALL)
    rows = P(ALL, None)
    mats = P(ALL, None, None)
    return jax.shard_map(
        body,
        mesh=halves,
        in_specs=(rows, rows, rows, P(), mats, mats, mats),
        out_specs=rows,
        check_vma=False,
    )
```

```python
import jax
import jax.numpy as jnp
from jax import lax
from jax.experimental import pallas as pl
from jax.experimental.pallas import tpu as pltpu
from jax.sharding import Mesh
from jax.sharding import PartitionSpec as P

BF = jnp.bfloat16
F32 = jnp.float32
ALL = ("z", "core", "local")
HALF = ("z", "local")
CAPS = (24, 32, 40)
SLOTS = 8
NARROW, WIDE = 256, 1024


def dot(a, b):
    return jnp.dot(a, b, preferred_element_type=F32)


def ranks(weights):
    named = weights > 0
    tokens = weights.shape[1]
    earlier = lax.broadcasted_iota(jnp.int32, (tokens, tokens), 0) < lax.broadcasted_iota(jnp.int32, (tokens, tokens), 1)
    rank = dot(named.astype(BF), earlier.astype(BF)).astype(jnp.int32)
    return jnp.where(named, rank, -1)


def slot_matrix(places, values, size):
    holders, tokens = places[0].shape
    slots = lax.broadcasted_iota(jnp.int32, (holders, size, tokens), 1)
    out = jnp.zeros((), BF)
    for place, value in zip(places, values):
        out = jnp.where(place[:, None, :] == slots, value[:, None, :], out)
    return out.reshape(holders * size, tokens)


def exchange(rows):
    return lax.all_to_all(rows, HALF, split_axis=0, concat_axis=0, tiled=True)


def after(x, *others):
    return lax.optimization_barrier((x, others))[0]


def hidden_of(gate, up):
    return jax.nn.silu(gate) * up


def expert_kernel(flags, rows, mask, *refs):
    sources, out, mats, hidden, sems = refs[:6], refs[6], refs[7:10], refs[10], refs[11]
    step = pl.program_id(0)
    kind = flags[step]
    count, width = hidden.shape[1], rows.shape[2]
    gate, up, down = mats

    def copy(i):
        return pltpu.make_async_copy(sources[i], mats[i % 3].at[i // 3], sems.at[i])

    @pl.when(step == 0)
    def _():
        for i in (0, 1, 3, 4, 2, 5):
            copy(i).start()

    @pl.loop(0, 2)
    def _(expert):
        @pl.when(step == 0)
        def _():
            for i in (0, 1):
                pltpu.make_async_copy(sources[i], mats[i].at[expert], sems.at[3 * expert + i]).wait()

        @pl.when((kind == expert + 1) | (kind == 3))
        def _():
            mine = (mask[0][:, :1] > 0) == (expert == 0)

            @pl.loop(0, hidden.shape[2] // NARROW)
            def _(j):
                cols = pl.ds(pl.multiple_of(j * NARROW, NARROW), NARROW)
                x = rows[...].reshape(count, width)
                act = hidden_of(dot(x, gate[expert, :, cols]), dot(x, up[expert, :, cols]))
                hidden[expert, :, cols] = jnp.where(mine, act, 0.0).astype(BF)

    @pl.when(step == 0)
    def _():
        copy(2).wait()
        copy(5).wait()

    def write(product):
        @pl.loop(0, width // WIDE)
        def _(j):
            cols = pl.ds(pl.multiple_of(j * WIDE, WIDE), WIDE)
            out[:, :, cols] = product(cols).astype(BF).reshape(out.shape[0], out.shape[1], WIDE)

    def one(expert):
        return lambda cols: dot(hidden[expert], down[expert, :, cols])

    @pl.when(kind == 0)
    def _():
        out[...] = jnp.zeros_like(out)

    pl.when((kind == 1) | (kind == 2))(lambda: write(one(jnp.maximum(kind, 1) - 1)))
    pl.when(kind == 3)(lambda: write(lambda cols: one(0)(cols) + one(1)(cols)))


def tile_plan(first_rows, all_rows, cap):
    sources, tiles, lanes = first_rows.shape[0], cap // SLOTS, 128
    slots = lax.broadcasted_iota(jnp.int32, (tiles, sources, SLOTS), 0) * SLOTS
    slots = slots + lax.broadcasted_iota(jnp.int32, (tiles, sources, SLOTS), 2)
    is_first = (slots < first_rows[None, :, None]).reshape(tiles, sources * SLOTS)
    any_row = (slots < all_rows[None, :, None]).reshape(tiles, sources * SLOTS)
    flags = jnp.any(is_first, axis=1).astype(jnp.int32) + 2 * jnp.any(any_row & ~is_first, axis=1).astype(jnp.int32)
    return flags, jnp.broadcast_to(is_first.astype(F32)[:, :, None], (tiles, sources * SLOTS, lanes))


def two_experts(flags, mask, rows, first, second):
    sources, cap, width = rows.shape
    ff = first[0].shape[1]
    count = sources * SLOTS
    block = pl.BlockSpec((sources, SLOTS, width), lambda i, f: (0, i, 0))
    return pl.pallas_call(
        expert_kernel,
        out_shape=pltpu.HBM(rows.shape, BF),
        grid_spec=pltpu.PrefetchScalarGridSpec(
            num_scalar_prefetch=1,
            grid=(cap // SLOTS,),
            in_specs=[block, pl.BlockSpec((1,) + mask.shape[1:], lambda i, f: (i, 0, 0))]
            + [pl.BlockSpec(memory_space=pl.ANY)] * 6,
            out_specs=block,
            scratch_shapes=[pltpu.VMEM((2,) + m.shape, BF) for m in first]
            + [pltpu.VMEM((2, count, ff), BF), pltpu.SemaphoreType.DMA((6,))],
        ),
        compiler_params=pltpu.CompilerParams(vmem_limit_bytes=40 * 2**20),
        cost_estimate=pl.CostEstimate(
            flops=6 * sources * cap * width * ff, bytes_accessed=12 * width * ff + 4 * sources * cap * width, transcendentals=0
        ),
    )(flags, rows, mask, *first, *second)


def body(tokens, expert_ids, gate_weights, slot_map, w_gate, w_up, w_down):
    tok, width = tokens.shape
    zs, locals_ = lax.axis_size("z"), lax.axis_size("local")
    chips = zs * locals_
    experts = slot_map.shape[0]
    z, core, local = (lax.axis_index(a) for a in ALL)
    full = 2 * (3 * tok // locals_)

    own = (w_gate[0], w_up[0], w_down[0])
    sib = tuple(lax.ppermute(m, "core", [(0, 1), (1, 0)]) for m in own)

    expert_rows = jnp.arange(experts, dtype=jnp.int32)
    ids, gates = expert_ids.T, gate_weights.T.astype(F32)
    spread = jnp.sum(jnp.where(ids[:, None, :] == expert_rows[:, None], gates[:, None, :], 0.0), axis=0).astype(BF)
    holder = (expert_rows // locals_) * locals_ + slot_map
    place = (expert_rows[:, None] == holder[None, :]).astype(BF)
    by_holder = dot(place, spread).astype(BF)
    counts = jnp.sum((by_holder > 0).astype(jnp.int32), axis=1)
    my_need = jnp.max(jnp.sum(counts.reshape(zs, 2, locals_), axis=1))
    message = jnp.stack([counts, jnp.broadcast_to(my_need, counts.shape)])
    table = lax.all_to_all(
        jnp.broadcast_to(message[None], (chips, 2, experts)), HALF, split_axis=0, concat_axis=0, tiled=True
    )
    need = jnp.max(table[:, 1])

    by_core = by_holder.reshape(zs, 2, locals_, tok)
    even, odd = (by_core[:, i].reshape(chips, tok) for i in (0, 1))
    weights = [jnp.where(core == 0, even, odd), jnp.where(core == 0, odd, even)]
    rank_own, rank_sib = ranks(weights[0]), ranks(weights[1])
    own_count = jnp.sum((rank_own >= 0).astype(jnp.int32), axis=1, keepdims=True)
    places = [rank_own, jnp.where(rank_sib >= 0, rank_sib + own_count, -1)]

    cells = table[:, 0]
    node = z * 2 + core
    own_rows, sib_rows = (
        jnp.sum(jnp.where(expert_rows == n * locals_ + local, cells, 0), axis=1) for n in (node, node + 1 - 2 * core)
    )
    all_rows = own_rows + sib_rows

    def layer(cap):
        def run(tokens, places, weights, own_rows, all_rows, own, sib):
            spread = slot_matrix(places, weights, cap)
            flags, mask = tile_plan(own_rows, all_rows, cap)
            send = dot(slot_matrix(places, [jnp.ones_like(w) for w in weights], cap), tokens).astype(BF)
            send, spread, flags, mask, sib = lax.optimization_barrier((send, spread, flags, mask, sib))
            out = two_experts(flags, mask, exchange(send.reshape(chips, cap, width)), own, sib)
            return dot(spread.T, exchange(out).reshape(-1, width)).astype(BF)

        return run

    caps = [c for c in CAPS if c < full] + [full]
    which = sum((need > c).astype(jnp.int32) for c in caps[:-1])
    return lax.switch(which, [layer(c) for c in caps], tokens, places, weights, own_rows, all_rows, own, sib)


def solution(mesh):
    halves = Mesh(mesh.devices.reshape(-1, 2, mesh.devices.shape[1]), ALL)
    rows = P(ALL, None)
    mats = P(ALL, None, None)
    return jax.shard_map(
        body,
        mesh=halves,
        in_specs=(rows, rows, rows, P(), mats, mats, mats),
        out_specs=rows,
        check_vma=False,
    )
```

```python
import jax
import jax.numpy as jnp
from jax import lax
from jax.experimental import pallas as pl
from jax.experimental.pallas import tpu as pltpu
from jax.sharding import Mesh
from jax.sharding import PartitionSpec as P

BF = jnp.bfloat16
F32 = jnp.float32
ALL = ("z", "core", "local")
HALF = ("z", "local")
CAPS = (24, 32, 40)
SLOTS = 8
NARROW, WIDE = 256, 1024


def dot(a, b):
    return jnp.dot(a, b, preferred_element_type=F32)


def ranks(weights):
    named = weights > 0
    tokens = weights.shape[1]
    earlier = lax.broadcasted_iota(jnp.int32, (tokens, tokens), 0) < lax.broadcasted_iota(jnp.int32, (tokens, tokens), 1)
    rank = dot(named.astype(BF), earlier.astype(BF)).astype(jnp.int32)
    return jnp.where(named, rank, -1)


def slot_matrix(places, values, size):
    holders, tokens = places[0].shape
    slots = lax.broadcasted_iota(jnp.int32, (holders, size, tokens), 1)
    out = jnp.zeros((), BF)
    for place, value in zip(places, values):
        out = jnp.where(place[:, None, :] == slots, value[:, None, :], out)
    return out.reshape(holders * size, tokens)


def exchange(rows):
    return lax.all_to_all(rows, HALF, split_axis=0, concat_axis=0, tiled=True)


def after(x, *others):
    return lax.optimization_barrier((x, others))[0]


def hidden_of(gate, up):
    return jax.nn.silu(gate) * up


def expert_kernel(flags, rows, mask, *refs):
    sources, out, mats, hidden, sems = refs[:6], refs[6], refs[7:10], refs[10], refs[11]
    step = pl.program_id(0)
    kind = flags[step]
    count, width = hidden.shape[1], rows.shape[2]
    gate, up, down = mats

    def copy(i):
        return pltpu.make_async_copy(sources[i], mats[i % 3].at[i // 3], sems.at[i])

    @pl.when(step == 0)
    def _():
        for i in (0, 1, 3, 4, 2, 5):
            copy(i).start()

    @pl.loop(0, 2)
    def _(expert):
        @pl.when(step == 0)
        def _():
            for i in (0, 1):
                pltpu.make_async_copy(sources[i], mats[i].at[expert], sems.at[3 * expert + i]).wait()

        @pl.when((kind == expert + 1) | (kind == 3))
        def _():
            mine = (mask[0][:, :1] > 0) == (expert == 0)

            @pl.loop(0, hidden.shape[2] // NARROW)
            def _(j):
                cols = pl.ds(pl.multiple_of(j * NARROW, NARROW), NARROW)
                x = rows[...].reshape(count, width)
                act = hidden_of(dot(x, gate[expert, :, cols]), dot(x, up[expert, :, cols]))
                hidden[expert, :, cols] = jnp.where(mine, act, 0.0).astype(BF)

    @pl.when(step == 0)
    def _():
        copy(2).wait()
        copy(5).wait()

    def write(product):
        @pl.loop(0, width // WIDE)
        def _(j):
            cols = pl.ds(pl.multiple_of(j * WIDE, WIDE), WIDE)
            out[:, :, cols] = product(cols).astype(BF).reshape(out.shape[0], out.shape[1], WIDE)

    def one(expert):
        return lambda cols: dot(hidden[expert], down[expert, :, cols])

    @pl.when(kind == 0)
    def _():
        out[...] = jnp.zeros_like(out)

    pl.when((kind == 1) | (kind == 2))(lambda: write(one(jnp.maximum(kind, 1) - 1)))
    pl.when(kind == 3)(lambda: write(lambda cols: one(0)(cols) + one(1)(cols)))


def tile_plan(first_rows, all_rows, cap):
    sources, tiles, lanes = first_rows.shape[0], cap // SLOTS, 128
    slots = lax.broadcasted_iota(jnp.int32, (tiles, sources, SLOTS), 0) * SLOTS
    slots = slots + lax.broadcasted_iota(jnp.int32, (tiles, sources, SLOTS), 2)
    is_first = (slots < first_rows[None, :, None]).reshape(tiles, sources * SLOTS)
    any_row = (slots < all_rows[None, :, None]).reshape(tiles, sources * SLOTS)
    flags = jnp.any(is_first, axis=1).astype(jnp.int32) + 2 * jnp.any(any_row & ~is_first, axis=1).astype(jnp.int32)
    return flags, jnp.broadcast_to(is_first.astype(F32)[:, :, None], (tiles, sources * SLOTS, lanes))


def two_experts(flags, mask, rows, first, second):
    sources, cap, width = rows.shape
    ff = first[0].shape[1]
    count = sources * SLOTS
    block = pl.BlockSpec((sources, SLOTS, width), lambda i, f: (0, i, 0))
    return pl.pallas_call(
        expert_kernel,
        out_shape=pltpu.HBM(rows.shape, BF),
        grid_spec=pltpu.PrefetchScalarGridSpec(
            num_scalar_prefetch=1,
            grid=(cap // SLOTS,),
            in_specs=[block, pl.BlockSpec((1,) + mask.shape[1:], lambda i, f: (i, 0, 0))]
            + [pl.BlockSpec(memory_space=pl.ANY)] * 6,
            out_specs=block,
            scratch_shapes=[pltpu.VMEM((2,) + m.shape, BF) for m in first]
            + [pltpu.VMEM((2, count, ff), BF), pltpu.SemaphoreType.DMA((6,))],
        ),
        compiler_params=pltpu.CompilerParams(vmem_limit_bytes=40 * 2**20),
        cost_estimate=pl.CostEstimate(
            flops=6 * sources * cap * width * ff, bytes_accessed=12 * width * ff + 4 * sources * cap * width, transcendentals=0
        ),
    )(flags, rows, mask, *first, *second)


def body(tokens, expert_ids, gate_weights, slot_map, w_gate, w_up, w_down):
    tok, width = tokens.shape
    zs, locals_ = lax.axis_size("z"), lax.axis_size("local")
    chips = zs * locals_
    experts = slot_map.shape[0]
    z, core, local = (lax.axis_index(a) for a in ALL)
    full = 2 * (3 * tok // locals_)

    own = (w_gate[0], w_up[0], w_down[0])
    sib = tuple(lax.ppermute(m, "core", [(0, 1), (1, 0)]) for m in own)

    expert_rows = jnp.arange(experts, dtype=jnp.int32)
    ids, gates = expert_ids.T, gate_weights.T.astype(F32)
    spread = jnp.sum(jnp.where(ids[:, None, :] == expert_rows[:, None], gates[:, None, :], 0.0), axis=0).astype(BF)
    holder = (expert_rows // locals_) * locals_ + slot_map
    place = (expert_rows[:, None] == holder[None, :]).astype(BF)
    by_holder = dot(place, spread).astype(BF)
    counts = jnp.sum((by_holder > 0).astype(jnp.int32), axis=1)
    my_need = jnp.max(jnp.sum(counts.reshape(zs, 2, locals_), axis=1))
    message = jnp.stack([counts, jnp.broadcast_to(my_need, counts.shape)])
    table = lax.all_to_all(
        jnp.broadcast_to(message[None], (chips, 2, experts)), HALF, split_axis=0, concat_axis=0, tiled=True
    )
    need = jnp.max(table[:, 1])

    by_core = by_holder.reshape(zs, 2, locals_, tok)
    even, odd = (by_core[:, i].reshape(chips, tok) for i in (0, 1))
    weights = [jnp.where(core == 0, even, odd), jnp.where(core == 0, odd, even)]
    rank_own, rank_sib = ranks(weights[0]), ranks(weights[1])
    own_count = jnp.sum((rank_own >= 0).astype(jnp.int32), axis=1, keepdims=True)
    places = [rank_own, jnp.where(rank_sib >= 0, rank_sib + own_count, -1)]

    cells = table[:, 0]
    node = z * 2 + core
    own_rows, sib_rows = (
        jnp.sum(jnp.where(expert_rows == n * locals_ + local, cells, 0), axis=1) for n in (node, node + 1 - 2 * core)
    )
    all_rows = own_rows + sib_rows

    def layer(cap):
        def run(tokens, places, weights, own_rows, all_rows, own, sib):
            spread = slot_matrix(places, weights, cap)
            flags, mask = tile_plan(own_rows, all_rows, cap)
            send = dot(slot_matrix(places, [jnp.ones_like(w) for w in weights], cap), tokens).astype(BF)
            send, spread, flags, mask, sib = lax.optimization_barrier((send, spread, flags, mask, sib))
            out = two_experts(flags, mask, exchange(send.reshape(chips, cap, width)), own, sib)
            return dot(spread.T, exchange(out).reshape(-1, width)).astype(BF)

        return run

    small, common, large = CAPS
    which = jnp.where(need > large, 2, jnp.where(need > common, 0, 1))
    operands = (tokens, places, weights, own_rows, all_rows, own, sib)

    def others(*args):
        return lax.switch(which, [layer(large), layer(common), layer(full)], *args)

    return lax.cond(need <= small, layer(small), others, *operands)


def solution(mesh):
    halves = Mesh(mesh.devices.reshape(-1, 2, mesh.devices.shape[1]), ALL)
    rows = P(ALL, None)
    mats = P(ALL, None, None)
    return jax.shard_map(
        body,
        mesh=halves,
        in_specs=(rows, rows, rows, P(), mats, mats, mats),
        out_specs=rows,
        check_vma=False,
    )
```

```python
import jax
import jax.numpy as jnp
from jax import lax
from jax.experimental import pallas as pl
from jax.experimental.pallas import tpu as pltpu
from jax.sharding import Mesh
from jax.sharding import PartitionSpec as P

BF = jnp.bfloat16
F32 = jnp.float32
ALL = ("z", "core", "local")
HALF = ("z", "local")
CAPS = (32, 40)
SLOTS = 8
NARROW, WIDE = 256, 1024


def dot(a, b):
    return jnp.dot(a, b, preferred_element_type=F32)


def ranks(weights):
    named = weights > 0
    tokens = weights.shape[1]
    earlier = lax.broadcasted_iota(jnp.int32, (tokens, tokens), 0) < lax.broadcasted_iota(jnp.int32, (tokens, tokens), 1)
    rank = dot(named.astype(BF), earlier.astype(BF)).astype(jnp.int32)
    return jnp.where(named, rank, -1)


def slot_matrix(places, values, size):
    holders, tokens = places[0].shape
    slots = lax.broadcasted_iota(jnp.int32, (holders, size, tokens), 1)
    out = jnp.zeros((), BF)
    for place, value in zip(places, values):
        out = jnp.where(place[:, None, :] == slots, value[:, None, :], out)
    return out.reshape(holders * size, tokens)


def exchange(rows):
    return lax.all_to_all(rows, HALF, split_axis=0, concat_axis=0, tiled=True)


def after(x, *others):
    return lax.optimization_barrier((x, others))[0]


def hidden_of(gate, up):
    return jax.nn.silu(gate) * up


def expert_kernel(flags, rows, mask, *refs):
    sources, out, mats, hidden, sems = refs[:6], refs[6], refs[7:10], refs[10], refs[11]
    step = pl.program_id(0)
    kind = flags[step]
    count, width = hidden.shape[1], rows.shape[2]
    gate, up, down = mats

    def copy(i):
        return pltpu.make_async_copy(sources[i], mats[i % 3].at[i // 3], sems.at[i])

    @pl.when(step == 0)
    def _():
        for i in (0, 1, 3, 4, 2, 5):
            copy(i).start()

    @pl.loop(0, 2)
    def _(expert):
        @pl.when(step == 0)
        def _():
            for i in (0, 1):
                pltpu.make_async_copy(sources[i], mats[i].at[expert], sems.at[3 * expert + i]).wait()

        @pl.when((kind == expert + 1) | (kind == 3))
        def _():
            mine = (mask[0][:, :1] > 0) == (expert == 0)

            @pl.loop(0, hidden.shape[2] // NARROW)
            def _(j):
                cols = pl.ds(pl.multiple_of(j * NARROW, NARROW), NARROW)
                x = rows[...].reshape(count, width)
                act = hidden_of(dot(x, gate[expert, :, cols]), dot(x, up[expert, :, cols]))
                hidden[expert, :, cols] = jnp.where(mine, act, 0.0).astype(BF)

    @pl.when(step == 0)
    def _():
        copy(2).wait()
        copy(5).wait()

    def write(product):
        @pl.loop(0, width // WIDE)
        def _(j):
            cols = pl.ds(pl.multiple_of(j * WIDE, WIDE), WIDE)
            out[:, :, cols] = product(cols).astype(BF).reshape(out.shape[0], out.shape[1], WIDE)

    def one(expert):
        return lambda cols: dot(hidden[expert], down[expert, :, cols])

    @pl.when(kind == 0)
    def _():
        out[...] = jnp.zeros_like(out)

    pl.when((kind == 1) | (kind == 2))(lambda: write(one(jnp.maximum(kind, 1) - 1)))
    pl.when(kind == 3)(lambda: write(lambda cols: one(0)(cols) + one(1)(cols)))


def tile_plan(first_rows, all_rows, cap):
    sources, tiles, lanes = first_rows.shape[0], cap // SLOTS, 128
    slots = lax.broadcasted_iota(jnp.int32, (tiles, sources, SLOTS), 0) * SLOTS
    slots = slots + lax.broadcasted_iota(jnp.int32, (tiles, sources, SLOTS), 2)
    is_first = (slots < first_rows[None, :, None]).reshape(tiles, sources * SLOTS)
    any_row = (slots < all_rows[None, :, None]).reshape(tiles, sources * SLOTS)
    flags = jnp.any(is_first, axis=1).astype(jnp.int32) + 2 * jnp.any(any_row & ~is_first, axis=1).astype(jnp.int32)
    return flags, jnp.broadcast_to(is_first.astype(F32)[:, :, None], (tiles, sources * SLOTS, lanes))


def two_experts(flags, mask, rows, first, second):
    sources, cap, width = rows.shape
    ff = first[0].shape[1]
    count = sources * SLOTS
    block = pl.BlockSpec((sources, SLOTS, width), lambda i, f: (0, i, 0))
    return pl.pallas_call(
        expert_kernel,
        out_shape=pltpu.HBM(rows.shape, BF),
        grid_spec=pltpu.PrefetchScalarGridSpec(
            num_scalar_prefetch=1,
            grid=(cap // SLOTS,),
            in_specs=[block, pl.BlockSpec((1,) + mask.shape[1:], lambda i, f: (i, 0, 0))]
            + [pl.BlockSpec(memory_space=pl.ANY)] * 6,
            out_specs=block,
            scratch_shapes=[pltpu.VMEM((2,) + m.shape, BF) for m in first]
            + [pltpu.VMEM((2, count, ff), BF), pltpu.SemaphoreType.DMA((6,))],
        ),
        compiler_params=pltpu.CompilerParams(vmem_limit_bytes=40 * 2**20),
        cost_estimate=pl.CostEstimate(
            flops=6 * sources * cap * width * ff, bytes_accessed=12 * width * ff + 4 * sources * cap * width, transcendentals=0
        ),
    )(flags, rows, mask, *first, *second)


def body(tokens, expert_ids, gate_weights, slot_map, w_gate, w_up, w_down):
    tok, width = tokens.shape
    zs, locals_ = lax.axis_size("z"), lax.axis_size("local")
    chips = zs * locals_
    experts = slot_map.shape[0]
    z, core, local = (lax.axis_index(a) for a in ALL)
    full = 2 * (3 * tok // locals_)

    own = (w_gate[0], w_up[0], w_down[0])
    sib = tuple(lax.ppermute(m, "core", [(0, 1), (1, 0)]) for m in own)

    expert_rows = jnp.arange(experts, dtype=jnp.int32)
    ids, gates = expert_ids.T, gate_weights.T.astype(F32)
    spread = jnp.sum(jnp.where(ids[:, None, :] == expert_rows[:, None], gates[:, None, :], 0.0), axis=0).astype(BF)
    holder = (expert_rows // locals_) * locals_ + slot_map
    place = (expert_rows[:, None] == holder[None, :]).astype(BF)
    by_holder = dot(place, spread).astype(BF)
    counts = jnp.sum((by_holder > 0).astype(jnp.int32), axis=1)
    my_need = jnp.max(jnp.sum(counts.reshape(zs, 2, locals_), axis=1))
    message = jnp.stack([counts, jnp.broadcast_to(my_need, counts.shape)])
    table = lax.all_to_all(
        jnp.broadcast_to(message[None], (chips, 2, experts)), HALF, split_axis=0, concat_axis=0, tiled=True
    )
    need = jnp.max(table[:, 1])

    by_core = by_holder.reshape(zs, 2, locals_, tok)
    even, odd = (by_core[:, i].reshape(chips, tok) for i in (0, 1))
    weights = [jnp.where(core == 0, even, odd), jnp.where(core == 0, odd, even)]
    rank_own, rank_sib = ranks(weights[0]), ranks(weights[1])
    own_count = jnp.sum((rank_own >= 0).astype(jnp.int32), axis=1, keepdims=True)
    places = [rank_own, jnp.where(rank_sib >= 0, rank_sib + own_count, -1)]

    cells = table[:, 0]
    node = z * 2 + core
    own_rows, sib_rows = (
        jnp.sum(jnp.where(expert_rows == n * locals_ + local, cells, 0), axis=1) for n in (node, node + 1 - 2 * core)
    )
    all_rows = own_rows + sib_rows

    def layer(cap):
        def run(tokens, places, weights, own_rows, all_rows, own, sib):
            spread = slot_matrix(places, weights, cap)
            flags, mask = tile_plan(own_rows, all_rows, cap)
            send = dot(slot_matrix(places, [jnp.ones_like(w) for w in weights], cap), tokens).astype(BF)
            send, spread, flags, mask, sib = lax.optimization_barrier((send, spread, flags, mask, sib))
            out = two_experts(flags, mask, exchange(send.reshape(chips, cap, width)), own, sib)
            return dot(spread.T, exchange(out).reshape(-1, width)).astype(BF)

        return run

    common, large = CAPS
    which = jnp.where(need > large, 2, jnp.where(need > common, 0, 1))
    operands = (tokens, places, weights, own_rows, all_rows, own, sib)
    return lax.switch(which, [layer(large), layer(common), layer(full)], *operands)


def solution(mesh):
    halves = Mesh(mesh.devices.reshape(-1, 2, mesh.devices.shape[1]), ALL)
    rows = P(ALL, None)
    mats = P(ALL, None, None)
    return jax.shard_map(
        body,
        mesh=halves,
        in_specs=(rows, rows, rows, P(), mats, mats, mats),
        out_specs=rows,
        check_vma=False,
    )
```
